32 devices in a mesh: parts: 2 (over y), tensor: 4 (over z), dp: 4 (over x, core).
Axes of the slice: x: 2, y: 2, z: 4, core: 2. Of those that a mesh axis runs over, the one named last changes fastest.
Arguments:
- layer_input: bfloat16 [2048, 4096], P(('parts', 'tensor'), 'dp'), parts along dimension 0, may hold values from -6 to 6
- gate_pre: bfloat16 [2048, 16384], P(('parts', 'dp'), 'tensor'), parts along dimension 0, may hold values from -8 to 8
- up_pre: bfloat16 [2048, 16384], P(('parts', 'dp'), 'tensor'), parts along dimension 0, may hold values from -6 to 6
- d_hidden: bfloat16 [2048, 16384], P(('parts', 'dp'), 'tensor'), parts along dimension 0, may hold values from -2 to 2
- w_gate: bfloat16 [4096, 16384], P('dp', 'tensor'), may hold values from -0.09375 to 0.09375
- w_up: bfloat16 [4096, 16384], P('dp', 'tensor'), may hold values from -0.09375 to 0.09375
- mask_gate: int32 [32, 128], P('dp', 'tensor'), may hold values 0 or 1
- mask_up: int32 [32, 128], P('dp', 'tensor'), may hold values 0 or 1
- lengths: int32 [8], P('parts'), parts along dimension 0, may hold values from 112 to 256, as said below
Outputs:
- input_grad: bfloat16 [2048, 4096], P(('parts', 'tensor'), 'dp'), parts along dimension 0
- grad_w_gate: bfloat16 [8192, 16384], P(('parts', 'dp'), 'tensor'), parts along dimension 0
- grad_w_up: bfloat16 [8192, 16384], P(('parts', 'dp'), 'tensor'), parts along dimension 0
The draws below stay inside these ranges and needn't reach their ends.
There are 2 independent parts, one for each index of `parts`. The reference program is written for one: setup_inputs(seed, part) draws one part's arguments, and reference() takes and returns one part's arrays. A program takes and returns all parts, laid end to end along the dimension named above; an argument that names none is the same for every part. Nothing has to cross between parts.
Inputs may be any that keep to these rules, and one draw needn't show every extreme that they name: Groups g and g + 4/2 form a pair whose lengths sum to at most 384; in every draw some group has all 256 slots used.
All inputs are finite; a program needn't handle non-finite values. No bound on the sum of `mask_gate` or of `mask_up` on one device may be relied on, other than what follows from the above.
Results may differ from the reference program's by a relative error of at most 0.0095.
Values may be sent and summed in bfloat16 or wider, within the bound.
A program may use at most 192 MiB of HBM per device.

```python
import jax
import jax.numpy as jnp
from jax import lax

D = 4096
FF = 16384
BLK = 128
TOK_DEV = 256
PAIR_MOST = 384
TOKENS = 1024
N_TENSOR = 4
N_DP = 4


def draw_lengths(key, part):
    key = jax.random.fold_in(key, 11)
    first_key, second_key, third_key = jax.random.split(key, 3)
    half = N_DP // 2
    heavy = jax.random.randint(first_key, (half,), PAIR_MOST - TOK_DEV, TOK_DEV + 1)
    heavy = heavy.at[0].set(TOK_DEV)
    shortfall = jax.random.randint(second_key, (half,), 0, TOK_DEV // 16 + 1)
    light = PAIR_MOST - heavy - shortfall
    flips = jax.random.randint(third_key, (half,), 0, 2)
    first = jnp.where(flips == 1, heavy, light)
    second = jnp.where(flips == 1, light, heavy)
    return jnp.concatenate([first, second]).astype(jnp.int32)


def place_ends(values, stream_key, least, top_value):
    spot = [jax.random.randint(jax.random.fold_in(stream_key, axis), (), 0, length) for axis, length in enumerate(values.shape)]
    main_axis = values.shape.index(max(values.shape))
    neighbour = spot[:main_axis] + [(spot[main_axis] + 1) % values.shape[main_axis]] + spot[main_axis + 1:]
    return values.at[tuple(spot)].set(least).at[tuple(neighbour)].set(top_value)


def spiked(entries, rng, source, target, parts, factor):
    def block_of(axis_at):
        return (jnp.arange(entries.shape[axis_at]) // (entries.shape[axis_at] // parts)).reshape((-1,) + (1,) * (entries.ndim - 1 - axis_at))

    one_side = jax.random.permutation(rng, parts)[block_of(target)]
    far = (block_of(target) + parts // 2) % parts
    return jnp.where((block_of(source) == one_side) | (block_of(source) == far), factor * entries, entries)


def block_levels(own_key, dims, cuts, smallest, high):
    level, own = 1.0, jax.random.fold_in(own_key, 6)
    for axis_at, parts in cuts:
        heights = jnp.exp(jax.random.uniform(jax.random.fold_in(own, axis_at), (parts,), jnp.float32, smallest / len(cuts), high / len(cuts)))
        level = level * jnp.repeat(heights, dims[axis_at] // parts).reshape([-1 if axis == axis_at else 1 for axis in range(len(dims))])
    return level


def noise(rng, extent, spread, limit, cuts=(), kind=jnp.bfloat16):
    entries = jax.random.normal(rng, extent, jnp.float32) * spread
    if len(cuts) > 0:
        entries = block_levels(rng, extent, cuts, -0.22, 0.18) * entries
    return jnp.clip(entries, min=-limit, max=limit).astype(kind)


def bell_draw_with(own_key, shape, scale, most, cuts, heavy, held_as=jnp.bfloat16):
    values = scale * jax.random.normal(own_key, shape, jnp.float32)
    if cuts:
        values = values * block_levels(own_key, shape, cuts, -0.22, 0.18)
    return jnp.clip(spiked(values, jax.random.fold_in(own_key, 3), *heavy), -most, most).astype(held_as)


def setup_inputs(seed: int = 0, part: int = 0) -> dict:
    arg_keys = jax.random.split(jax.random.key(seed), 10)
    part_keys = jax.random.split(jax.random.fold_in(arg_keys[9], part), 10)
    layer_input = noise(part_keys[0], (TOKENS, D), 1.0, 6.0, ((0, 4), (1, 4)))
    gate_pre = noise(part_keys[1], (TOKENS, FF), 1.5, 8.0, ((0, 4), (1, 4)))
    up_pre = noise(part_keys[2], (TOKENS, FF), 1.0, 6.0, ((0, 4), (1, 4)))
    d_hidden = bell_draw_with(part_keys[3], (TOKENS, FF), 0.25, 2.0, ((0, 4), (1, 4)), (1, 0, 4, 2.0))
    w_gate = noise(arg_keys[4], (D, FF), D ** -0.5, 0.09375, ((0, 4), (1, 4)))
    w_up = noise(arg_keys[5], (D, FF), D ** -0.5, 0.09375, ((0, 4), (1, 4)))
    mask_gate = place_ends((jax.random.randint(arg_keys[6], (D // BLK, FF // BLK), 0, 2) < 1).astype(jnp.int32), jax.random.fold_in(arg_keys[6], 1), 0, 1)
    mask_up = place_ends((jax.random.randint(arg_keys[7], (D // BLK, FF // BLK), 0, 2) < 1).astype(jnp.int32), jax.random.fold_in(arg_keys[7], 1), 0, 1)
    lengths = draw_lengths(jax.random.fold_in(jax.random.fold_in(arg_keys[9], part), 71), part)
    return dict(layer_input=layer_input, gate_pre=gate_pre, up_pre=up_pre, d_hidden=d_hidden, w_gate=w_gate, w_up=w_up, mask_gate=mask_gate, mask_up=mask_up, lengths=lengths)


def expand(mask):
    return jnp.repeat(jnp.repeat(mask, BLK, axis=0), BLK, axis=1)


def swiglu_back(gate, upper, grad, keep):
    g = gate.astype(jnp.float32)
    sig = jax.nn.sigmoid(g)
    err = jnp.where(keep[:, None], grad.astype(jnp.float32), jnp.float32(0.0))
    d_up = err * g * sig
    d_gate = err * upper.astype(jnp.float32) * sig * (1.0 + g * (1.0 - sig))
    return d_gate.astype(jnp.bfloat16), d_up.astype(jnp.bfloat16)


def reference(layer_input, gate_pre, up_pre, d_hidden, w_gate, w_up, mask_gate, mask_up, lengths):
    slots = jnp.arange(TOKENS, dtype=jnp.int32)
    keep = (slots % TOK_DEV) < lengths[slots // TOK_DEV]
    d_gate, d_up = swiglu_back(gate_pre, up_pre, d_hidden, keep)
    keep_gate = expand(mask_gate).astype(jnp.bfloat16)
    keep_up = expand(mask_up).astype(jnp.bfloat16)
    gate_eff = w_gate * keep_gate
    up_eff = w_up * keep_up
    contract = (((0,), (0,)), ((), ()))
    grad_w_gate = lax.dot_general(layer_input, d_gate, contract, preferred_element_type=jnp.float32)
    grad_w_gate = (grad_w_gate * keep_gate.astype(jnp.float32)).astype(jnp.bfloat16)
    grad_w_up = lax.dot_general(layer_input, d_up, contract, preferred_element_type=jnp.float32)
    grad_w_up = (grad_w_up * keep_up.astype(jnp.float32)).astype(jnp.bfloat16)
    width = FF // N_TENSOR

    def shards(array):
        return jnp.moveaxis(array.reshape(array.shape[0], N_TENSOR, width), 1, 0)

    inner = (((1,), (1,)), ((), ()))

    def step(total, pieces):
        grad_g, grad_u, weight_g, weight_u = pieces
        term = lax.dot_general(grad_g, weight_g, inner, preferred_element_type=jnp.float32)
        term = term + lax.dot_general(grad_u, weight_u, inner, preferred_element_type=jnp.float32)
        return total + term.astype(jnp.bfloat16).astype(jnp.float32), None

    start = jnp.zeros((TOKENS, D), jnp.float32)
    total, _ = lax.scan(step, start, (shards(d_gate), shards(d_up), shards(gate_eff), shards(up_eff)))
    return total.astype(jnp.bfloat16), grad_w_gate, grad_w_up
```

```python
import functools

import jax
import jax.numpy as jnp
from jax import lax
from jax.experimental import pallas as pl
from jax.experimental.pallas import tpu as pltpu
from jax.sharding import PartitionSpec as P

BLK = 128
STAGES = 4
CORES = 2
VMEM_LIMIT = 60 * 2**20
MESH = pl.DeviceIdType.MESH
NT = (((1,), (1,)), ((), ()))


def gather_kernel(
    x_in, gate_in, up_in, dh_in, wg_in, wu_in, mg_in, mu_in, len_in,
    summed, dg_out, du_out, xt_out, kg_out, ku_out,
    dg, du, wg, wu, gate, up, dh, xs, term, part,
    load_sem, w_sem, x_sem, xsend, xrecv, psend, precv, ssend, srecv, fsend, frecv, out_sem, rsend, rrecv,
):
    t = lax.axis_index("tensor")
    i = lax.axis_index("dp")
    n_t = xs.shape[0] * xs.shape[2]
    chip, core = i // CORES, i % CORES
    far = 1 - chip
    sib = chip * CORES + (1 - core)
    pair = far * CORES + core
    stages, rows, ff = gate.shape
    feats = wg.shape[0]

    loads = []
    for r in range(stages):
        loads.append([
            pltpu.make_async_copy(src.at[r], dst.at[r], load_sem.at[r, k])
            for k, (src, dst) in enumerate(((gate_in, gate), (up_in, up), (dh_in, dh)))
        ])
        for copy in loads[-1]:
            copy.start()
    w_loads = [
        pltpu.make_async_copy(wg_in, wg, w_sem.at[0]),
        pltpu.make_async_copy(wu_in, wu, w_sem.at[1]),
    ]
    for copy in w_loads:
        copy.start()
    own_x = pltpu.make_async_copy(x_in, xs.at[t // CORES, :, t % CORES], x_sem)
    own_x.start()

    barrier = pltpu.get_barrier_semaphore()
    for peer in (sib, pair):
        pl.semaphore_signal(barrier, inc=1, device_id={"dp": peer}, device_id_type=MESH)
    for k in range(1, n_t):
        pl.semaphore_signal(barrier, inc=1, device_id={"tensor": (t + k) % n_t}, device_id_type=MESH)
    pl.semaphore_wait(barrier, n_t + 1)

    x_copies = []
    for k in range(1, n_t):
        x_copies.append(pltpu.make_async_remote_copy(
            src_ref=x_in,
            dst_ref=xs.at[t // CORES, :, t % CORES],
            send_sem=xsend.at[k - 1],
            recv_sem=xrecv.at[k - 1],
            device_id={"tensor": (t + k) % n_t},
            device_id_type=MESH,
        ))
        x_copies[-1].start()

    used = len_in[i]
    p_copies, s_copies, f_copies = [], [], []
    tile = min(512, ff)
    for r in range(stages):
        for copy in loads[r]:
            copy.wait()

        @pl.loop(0, ff // tile)
        def _(c):
            cols = pl.ds(pl.multiple_of(c * tile, tile), tile)
            g = gate[r, :, cols].astype(jnp.float32)
            sig = jax.nn.sigmoid(g)
            slot = lax.broadcasted_iota(jnp.int32, (rows, tile), 0) + r * rows
            err = jnp.where(slot < used, dh[r, :, cols].astype(jnp.float32), jnp.float32(0.0))
            d_up = err * g * sig
            d_gate = err * up[r, :, cols].astype(jnp.float32) * sig * (1.0 + g * (1.0 - sig))
            dg[chip, r, core, :, cols] = d_gate.astype(jnp.bfloat16)
            du[chip, r, core, :, cols] = d_up.astype(jnp.bfloat16)

        for peer, send, recv, kept in ((pair, psend, precv, p_copies), (sib, ssend, srecv, s_copies)):
            kept.append([
                pltpu.make_async_remote_copy(
                    src_ref=d.at[chip, r, core],
                    dst_ref=d.at[chip, r, core],
                    send_sem=send.at[r, k],
                    recv_sem=recv.at[r, k],
                    device_id={"dp": peer},
                    device_id_type=MESH,
                )
                for k, d in enumerate((dg, du))
            ])
            for copy in kept[-1]:
                copy.start()

    blocks = mg_in.shape[1]
    spread = (
        lax.broadcasted_iota(jnp.int32, (blocks, ff), 1) // BLK
        == lax.broadcasted_iota(jnp.int32, (blocks, ff), 0)
    ).astype(jnp.float32)
    for m_in, k_out, w, load in ((mg_in, kg_out, wg, w_loads[0]), (mu_in, ku_out, wu, w_loads[1])):
        k_out[...] = jnp.dot(m_in[...].astype(jnp.float32), spread, preferred_element_type=jnp.float32)
        load.wait()

        @pl.loop(0, feats // BLK)
        def _(a):
            at = pl.ds(pl.multiple_of(a * BLK, BLK), BLK)
            w[at, :] = w[at, :] * k_out[pl.ds(a, 1), :].astype(jnp.bfloat16)

    out_copies = []

    def stage(where, r):
        for k, (d, d_out) in enumerate(((dg, dg_out), (du, du_out))):
            copy = pltpu.make_async_copy(d.at[where, r], d_out.at[where, r], out_sem.at[where, r, k])
            copy.start()
            out_copies.append(copy)
        wide = min(256, feats)

        @pl.loop(0, feats // wide)
        def _(n):
            at = pl.ds(pl.multiple_of(n * wide, wide), wide)
            total = lax.dot_general(
                dg[where, r].reshape(CORES * rows, ff), wg[at, :], NT, preferred_element_type=jnp.float32
            )
            total = total + lax.dot_general(
                du[where, r].reshape(CORES * rows, ff), wu[at, :], NT, preferred_element_type=jnp.float32
            )
            term[where, r, :, :, at] = total.astype(jnp.bfloat16).reshape(CORES, rows, wide)

        for c in range(CORES):
            owner = where * CORES + c

            @pl.when(owner != t)
            def _():
                pltpu.make_async_remote_copy(
                    src_ref=term.at[where, r, c],
                    dst_ref=part.at[t, r],
                    send_sem=rsend.at[owner, r],
                    recv_sem=rrecv.at[t, r],
                    device_id={"tensor": owner},
                    device_id_type=MESH,
                ).start()

    for r in range(stages):
        for copy in s_copies[r]:
            copy.wait_recv()
        stage(chip, r)

    for r in range(stages):
        for copy in p_copies[r]:
            copy.wait_recv()
        f_copies.append([
            pltpu.make_async_remote_copy(
                src_ref=d.at[far, r, core],
                dst_ref=d.at[far, r, core],
                send_sem=fsend.at[r, k],
                recv_sem=frecv.at[r, k],
                device_id={"dp": sib},
                device_id_type=MESH,
            )
            for k, d in enumerate((dg, du))
        ])
        for copy in f_copies[-1]:
            copy.start()
        for copy in f_copies[-1]:
            copy.wait_recv()
        stage(far, r)
        if r == stages - 2:
            own_x.wait()
            for copy in x_copies:
                copy.wait_recv()
            span = CORES * rows
            for a in range(xs.shape[0]):
                for b in range(stages):
                    at = (a * stages + b) * span
                    xt_out[:, at : at + span] = xs[a, b].reshape(span, feats).T

    for k in range(1, n_t):
        for r in range(stages):
            other = (t + k) % n_t
            copy = pltpu.make_async_remote_copy(
                src_ref=term.at[other // CORES, r, other % CORES],
                dst_ref=part.at[other, r],
                send_sem=rsend.at[other, r],
                recv_sem=rrecv.at[other, r],
                device_id={"tensor": other},
                device_id_type=MESH,
            )
            copy.wait_recv()
            copy.wait_send()
    for r in range(stages):
        total = term[t // CORES, r, t % CORES].astype(jnp.float32)
        for k in range(1, n_t):
            total = total + part[(t + k) % n_t, r].astype(jnp.float32)
        summed[r] = total.astype(jnp.bfloat16)

    for copy in x_copies:
        copy.wait_send()
    for kept in (p_copies, s_copies, f_copies):
        for copies in kept:
            for copy in copies:
                copy.wait_send()
    for copy in out_copies:
        copy.wait()


def weight_kernel(xt, dg, du, kg, ku, out_g, out_u):
    feats = xt.shape[0]
    high = 256
    for d, keep, out in ((dg, kg, out_g), (du, ku, out_u)):
        for a in range(feats // high):
            total = jnp.dot(xt[a * high : (a + 1) * high, :], d[...], preferred_element_type=jnp.float32)
            for b in range(high // BLK):
                row = a * (high // BLK) + b
                out[row * BLK : (row + 1) * BLK, :] = (
                    total[b * BLK : (b + 1) * BLK, :] * keep[row : row + 1, :]
                ).astype(jnp.bfloat16)


def staged(layer_input, gate_pre, up_pre, d_hidden, w_gate, w_up, mask_gate, mask_up, lengths):
    slots, ff = gate_pre.shape
    feats = w_gate.shape[0]
    chips = lengths.shape[0] // CORES
    rows = slots // STAGES
    n_t = chips * CORES
    bf16, f32 = jnp.bfloat16, jnp.float32
    tokens = chips * CORES * slots

    def cut(array):
        return array.reshape(STAGES, rows, array.shape[1])

    hbm = pl.BlockSpec(memory_space=pl.ANY)
    vmem = pl.BlockSpec(memory_space=pltpu.VMEM)
    dma = pltpu.SemaphoreType.DMA
    summed, dg, du, xt, kg, ku = pl.pallas_call(
        gather_kernel,
        out_shape=(
            jax.ShapeDtypeStruct((STAGES, rows, feats), bf16),
            jax.ShapeDtypeStruct((chips, STAGES, CORES, rows, ff), bf16),
            jax.ShapeDtypeStruct((chips, STAGES, CORES, rows, ff), bf16),
            jax.ShapeDtypeStruct((feats, tokens), bf16),
            jax.ShapeDtypeStruct((feats // BLK, ff), f32),
            jax.ShapeDtypeStruct((feats // BLK, ff), f32),
        ),
        in_specs=[hbm] * 6 + [vmem] * 2 + [pl.BlockSpec(memory_space=pltpu.SMEM)],
        out_specs=(vmem, hbm, hbm, vmem, vmem, vmem),
        scratch_shapes=[
            pltpu.VMEM((chips, STAGES, CORES, rows, ff), bf16),
            pltpu.VMEM((chips, STAGES, CORES, rows, ff), bf16),
            pltpu.VMEM((feats, ff), bf16),
            pltpu.VMEM((feats, ff), bf16),
            pltpu.VMEM((STAGES, rows, ff), bf16),
            pltpu.VMEM((STAGES, rows, ff), bf16),
            pltpu.VMEM((STAGES, rows, ff), bf16),
            pltpu.VMEM((chips, STAGES, CORES, rows, feats), bf16),
            pltpu.VMEM((chips, STAGES, CORES, rows, feats), bf16),
            pltpu.VMEM((n_t, STAGES, rows, feats), bf16),
            dma((STAGES, 3)), dma((2,)), dma, dma((n_t - 1,)), dma((n_t - 1,)),
            dma((STAGES, 2)), dma((STAGES, 2)), dma((STAGES, 2)), dma((STAGES, 2)),
            dma((STAGES, 2)), dma((STAGES, 2)), dma((chips, STAGES, 2)),
            dma((n_t, STAGES)), dma((n_t, STAGES)),
        ],
        compiler_params=pltpu.CompilerParams(
            collective_id=0, has_side_effects=True, vmem_limit_bytes=VMEM_LIMIT
        ),
        name="gather_and_input_grad",
    )(
        cut(layer_input), cut(gate_pre), cut(up_pre), cut(d_hidden),
        w_gate, w_up, mask_gate, mask_up, lengths,
    )
    wide = 512
    grad_w_gate, grad_w_up = pl.pallas_call(
        weight_kernel,
        grid=(ff // wide,),
        out_shape=(jax.ShapeDtypeStruct((feats, ff), bf16),) * 2,
        in_specs=[
            pl.BlockSpec((feats, tokens), lambda j: (0, 0)),
            pl.BlockSpec((tokens, wide), lambda j: (0, j)),
            pl.BlockSpec((tokens, wide), lambda j: (0, j)),
            pl.BlockSpec((feats // BLK, wide), lambda j: (0, j)),
            pl.BlockSpec((feats // BLK, wide), lambda j: (0, j)),
        ],
        out_specs=(pl.BlockSpec((feats, wide), lambda j: (0, j)),) * 2,
        compiler_params=pltpu.CompilerParams(vmem_limit_bytes=VMEM_LIMIT),
        name="weight_grads",
    )(xt, dg.reshape(tokens, ff), du.reshape(tokens, ff), kg, ku)
    return summed.reshape(slots, feats), grad_w_gate, grad_w_up


def expand(mask):
    return jnp.repeat(jnp.repeat(mask, BLK, axis=0), BLK, axis=1)


def swiglu_back(gate, upper, grad, keep):
    g = gate.astype(jnp.float32)
    sig = jax.nn.sigmoid(g)
    err = jnp.where(keep[:, None], grad.astype(jnp.float32), jnp.float32(0.0))
    d_up = err * g * sig
    d_gate = err * upper.astype(jnp.float32) * sig * (1.0 + g * (1.0 - sig))
    return (d_gate.astype(jnp.bfloat16), d_up.astype(jnp.bfloat16))


def local(layer_input, gate_pre, up_pre, d_hidden, w_gate, w_up, mask_gate, mask_up, lengths):
    group = lax.axis_index("dp")
    slots_dev = gate_pre.shape[0]
    keep_gate = expand(mask_gate).astype(jnp.bfloat16)
    keep_up = expand(mask_up).astype(jnp.bfloat16)
    gate_eff = w_gate * keep_gate
    up_eff = w_up * keep_up
    inner = (((1,), (1,)), ((), ()))
    input_all = lax.all_gather(layer_input, "tensor", axis=0, tiled=True)
    keep = jnp.arange(slots_dev) < lengths[group]
    d_gate, d_up = swiglu_back(gate_pre, up_pre, d_hidden, keep)
    gate_all, up_all = (
        lax.all_gather(d_gate, "dp", axis=0, tiled=True),
        lax.all_gather(d_up, "dp", axis=0, tiled=True),
    )
    term = lax.dot_general(gate_all, gate_eff, inner, preferred_element_type=jnp.float32)
    summed = lax.psum_scatter(
        (term + lax.dot_general(up_all, up_eff, inner, preferred_element_type=jnp.float32)).astype(
            jnp.bfloat16
        ),
        "tensor",
        scatter_dimension=0,
        tiled=True,
    )
    contract = (((0,), (0,)), ((), ()))
    grad_w_gate = lax.dot_general(input_all, gate_all, contract, preferred_element_type=jnp.float32)
    grad_w_gate = (grad_w_gate * keep_gate.astype(jnp.float32)).astype(jnp.bfloat16)
    grad_w_up = lax.dot_general(input_all, up_all, contract, preferred_element_type=jnp.float32)
    grad_w_up = (grad_w_up * keep_up.astype(jnp.float32)).astype(jnp.bfloat16)
    return (summed, grad_w_gate, grad_w_up)


def solution(mesh):
    placed = (
        P(("parts", "tensor"), "dp"),
        P(("parts", "dp"), "tensor"),
        P(("parts", "dp"), "tensor"),
        P(("parts", "dp"), "tensor"),
        P("dp", "tensor"),
        P("dp", "tensor"),
        P("dp", "tensor"),
        P("dp", "tensor"),
        P("parts"),
    )
    paired = mesh.shape["dp"] == 2 * CORES and mesh.shape["tensor"] == mesh.shape["dp"]
    return jax.shard_map(
        staged if paired else local,
        mesh=mesh,
        in_specs=placed,
        out_specs=(
            P(("parts", "tensor"), "dp"),
            P(("parts", "dp"), "tensor"),
            P(("parts", "dp"), "tensor"),
        ),
        check_vma=False,
    )
```

```python
import functools

import jax
import jax.numpy as jnp
from jax import lax
from jax.experimental import pallas as pl
from jax.experimental.pallas import tpu as pltpu
from jax.sharding import PartitionSpec as P

BLK = 128
STAGES = 4
EARLY = 2
CORES = 2
VMEM_LIMIT = 60 * 2**20
MESH = pl.DeviceIdType.MESH
NT = (((1,), (1,)), ((), ()))


def cuts(feats):
    half = feats // 2
    return [(r, 0, feats) for r in range(STAGES - 1)] + [(STAGES - 1, 0, half), (STAGES - 1, half, half)]


def gather_kernel(
    x_in, gate_in, up_in, dh_in, wg_in, wu_in, mg_in, mu_in, len_in,
    summed, dg_out, du_out, pg_out, pu_out, xt_out, kg_out, ku_out,
    dg, du, wg, wu, gate, up, dh, xs, xt, held, term, part,
    load_sem, w_sem, x_sem, xsend, xrecv, psend, precv, ssend, srecv, fsend, frecv, out_sem, held_sem, rsend, rrecv,
):
    t = lax.axis_index("tensor")
    i = lax.axis_index("dp")
    n_t = xs.shape[0] * xs.shape[2]
    chip, core = i // CORES, i % CORES
    far = 1 - chip
    sib = chip * CORES + (1 - core)
    pair = far * CORES + core
    stages, rows, ff = gate.shape
    feats = wg.shape[0]
    pieces = cuts(feats)

    loads = []
    for r in range(stages):
        loads.append([
            pltpu.make_async_copy(src.at[r], dst.at[r], load_sem.at[r, k])
            for k, (src, dst) in enumerate(((gate_in, gate), (up_in, up), (dh_in, dh)))
        ])
        for copy in loads[-1]:
            copy.start()
    w_loads = [
        pltpu.make_async_copy(wg_in, wg, w_sem.at[0]),
        pltpu.make_async_copy(wu_in, wu, w_sem.at[1]),
    ]
    for copy in w_loads:
        copy.start()
    own_x = pltpu.make_async_copy(x_in, xs.at[t // CORES, :, t % CORES], x_sem)
    own_x.start()

    barrier = pltpu.get_barrier_semaphore()
    for peer in (sib, pair):
        pl.semaphore_signal(barrier, inc=1, device_id={"dp": peer}, device_id_type=MESH)
    for k in range(1, n_t):
        pl.semaphore_signal(barrier, inc=1, device_id={"tensor": (t + k) % n_t}, device_id_type=MESH)
    pl.semaphore_wait(barrier, n_t + 1)

    x_copies = []
    for k in range(1, n_t):
        x_copies.append(pltpu.make_async_remote_copy(
            src_ref=x_in,
            dst_ref=xs.at[t // CORES, :, t % CORES],
            send_sem=xsend.at[k - 1],
            recv_sem=xrecv.at[k - 1],
            device_id={"tensor": (t + k) % n_t},
            device_id_type=MESH,
        ))
        x_copies[-1].start()

    used = len_in[i]
    p_copies, s_copies, f_copies = [], [], []
    tile = min(512, ff)
    for r in range(stages):
        for copy in loads[r]:
            copy.wait()

        @pl.loop(0, ff // tile)
        def _(c):
            cols = pl.ds(pl.multiple_of(c * tile, tile), tile)
            g = gate[r, :, cols].astype(jnp.float32)
            sig = jax.nn.sigmoid(g)
            slot = lax.broadcasted_iota(jnp.int32, (rows, tile), 0) + r * rows
            err = jnp.where(slot < used, dh[r, :, cols].astype(jnp.float32), jnp.float32(0.0))
            d_up = err * g * sig
            d_gate = err * up[r, :, cols].astype(jnp.float32) * sig * (1.0 + g * (1.0 - sig))
            dg[chip, r, core, :, cols] = d_gate.astype(jnp.bfloat16)
            du[chip, r, core, :, cols] = d_up.astype(jnp.bfloat16)

        for peer, send, recv, kept in ((pair, psend, precv, p_copies), (sib, ssend, srecv, s_copies)):
            kept.append([
                pltpu.make_async_remote_copy(
                    src_ref=d.at[chip, r, core],
                    dst_ref=d.at[chip, r, core],
                    send_sem=send.at[r, k],
                    recv_sem=recv.at[r, k],
                    device_id={"dp": peer},
                    device_id_type=MESH,
                )
                for k, d in enumerate((dg, du))
            ])
            for copy in kept[-1]:
                copy.start()

    blocks = mg_in.shape[1]
    spread = (
        lax.broadcasted_iota(jnp.int32, (blocks, ff), 1) // BLK
        == lax.broadcasted_iota(jnp.int32, (blocks, ff), 0)
    ).astype(jnp.float32)
    for m_in, k_out, w, load in ((mg_in, kg_out, wg, w_loads[0]), (mu_in, ku_out, wu, w_loads[1])):
        k_out[...] = jnp.dot(m_in[...].astype(jnp.float32), spread, preferred_element_type=jnp.float32)
        load.wait()

        @pl.loop(0, feats // BLK)
        def _(a):
            at = pl.ds(pl.multiple_of(a * BLK, BLK), BLK)
            w[at, :] = w[at, :] * k_out[pl.ds(a, 1), :].astype(jnp.bfloat16)

    out_copies = []

    def terms(where, first, last, low, many):
        wide = min(256, many)
        tall = (last - first) * CORES * rows

        @pl.loop(0, many // wide)
        def _(n):
            at = pl.ds(pl.multiple_of(low + n * wide, wide), wide)
            total = lax.dot_general(
                dg[where, first:last].reshape(tall, ff), wg[at, :], NT, preferred_element_type=jnp.float32
            )
            total = total + lax.dot_general(
                du[where, first:last].reshape(tall, ff), wu[at, :], NT, preferred_element_type=jnp.float32
            )
            term[where, first:last, :, :, at] = total.astype(jnp.bfloat16).reshape(
                last - first, CORES, rows, wide
            )

        for q, (r, start, length) in enumerate(pieces):
            if not (first <= r < last and low <= start < low + many):
                continue
            for c in range(CORES):
                owner = where * CORES + c

                @pl.when(owner != t)
                def _():
                    pltpu.make_async_remote_copy(
                        src_ref=term.at[where, r, c, :, start : start + length],
                        dst_ref=part.at[t, r, :, start : start + length],
                        send_sem=rsend.at[owner, q],
                        recv_sem=rrecv.at[t, q],
                        device_id={"tensor": owner},
                        device_id_type=MESH,
                    ).start()

    span = CORES * rows

    def partial(k, d, p_out):
        near, wide = stages * span, held.shape[2]
        steps = ff // wide

        def out(j):
            cols = pl.ds(pl.multiple_of(j * wide, wide), wide)
            return pltpu.make_async_copy(held.at[j % 2], p_out.at[:, cols], held_sem.at[k, j % 2])

        @pl.loop(0, steps)
        def _(j):
            @pl.when(j >= 2)
            def _():
                out(j - 2).wait()

            cols = pl.ds(pl.multiple_of(j * wide, wide), wide)
            total = jnp.dot(
                xt[:, :near], d[chip, :, :, :, cols].reshape(near, wide), preferred_element_type=jnp.float32
            )
            total = total + jnp.dot(
                xt[:, near:], d[far, :EARLY, :, :, cols].reshape(EARLY * span, wide),
                preferred_element_type=jnp.float32,
            )
            held[j % 2] = total.astype(jnp.bfloat16)
            out(j).start()

        for j in range(steps - 2, steps):
            out(j).wait()

    for r in range(stages):
        for copy in s_copies[r]:
            copy.wait_recv()
    terms(chip, 0, stages, 0, feats)

    for r in range(stages):
        for copy in p_copies[r]:
            copy.wait_recv()
        f_copies.append([
            pltpu.make_async_remote_copy(
                src_ref=d.at[far, r, core],
                dst_ref=d.at[far, r, core],
                send_sem=fsend.at[r, k],
                recv_sem=frecv.at[r, k],
                device_id={"dp": sib},
                device_id_type=MESH,
            )
            for k, d in enumerate((dg, du))
        ])
        for copy in f_copies[-1]:
            copy.start()
        for copy in f_copies[-1]:
            copy.wait_recv()
        if r >= EARLY:
            for k, (d, d_out) in enumerate(((dg, dg_out), (du, du_out))):
                copy = pltpu.make_async_copy(d.at[far, r], d_out.at[r - EARLY], out_sem.at[r - EARLY, k])
                copy.start()
                out_copies.append(copy)
        if r == EARLY - 1:
            terms(far, 0, EARLY, 0, feats)
            own_x.wait()
            for copy in x_copies:
                copy.wait_recv()
            for at, where in enumerate((chip, far)):
                for b in range(stages):
                    block = xs[where, b].reshape(span, feats).T
                    if at == 0 or b < EARLY:
                        first = (at * stages + b) * span
                        xt[:, first : first + span] = block
                    else:
                        first = (b - EARLY) * span
                        xt_out[:, first : first + span] = block
            partial(0, dg, pg_out)
        if EARLY <= r < stages - 1:
            terms(far, r, r + 1, 0, feats)
        if r == stages - 1:
            terms(far, r, r + 1, 0, feats // 2)
            terms(far, r, r + 1, feats // 2, feats // 2)
        if r == EARLY:
            partial(1, du, pu_out)

    for k in range(1, n_t):
        for q, (r, start, length) in enumerate(pieces):
            other = (t + k) % n_t
            copy = pltpu.make_async_remote_copy(
                src_ref=term.at[other // CORES, r, other % CORES, :, start : start + length],
                dst_ref=part.at[other, r, :, start : start + length],
                send_sem=rsend.at[other, q],
                recv_sem=rrecv.at[other, q],
                device_id={"tensor": other},
                device_id_type=MESH,
            )
            copy.wait_recv()
            copy.wait_send()
    for r in range(stages):
        total = term[t // CORES, r, t % CORES].astype(jnp.float32)
        for k in range(1, n_t):
            total = total + part[(t + k) % n_t, r].astype(jnp.float32)
        summed[r] = total.astype(jnp.bfloat16)

    for copy in x_copies:
        copy.wait_send()
    for kept in (p_copies, s_copies, f_copies):
        for copies in kept:
            for copy in copies:
                copy.wait_send()
    for copy in out_copies:
        copy.wait()


def weight_kernel(xt, dg, du, pg, pu, kg, ku, out_g, out_u):
    feats = xt.shape[0]
    high = 256
    for d, p, keep, out in ((dg, pg, kg, out_g), (du, pu, ku, out_u)):
        for a in range(feats // high):
            total = jnp.dot(xt[a * high : (a + 1) * high, :], d[...], preferred_element_type=jnp.float32)
            total = total + p[a * high : (a + 1) * high, :].astype(jnp.float32)
            for b in range(high // BLK):
                row = a * (high // BLK) + b
                out[row * BLK : (row + 1) * BLK, :] = (
                    total[b * BLK : (b + 1) * BLK, :] * keep[row : row + 1, :]
                ).astype(jnp.bfloat16)


def staged(layer_input, gate_pre, up_pre, d_hidden, w_gate, w_up, mask_gate, mask_up, lengths):
    slots, ff = gate_pre.shape
    feats = w_gate.shape[0]
    chips = lengths.shape[0] // CORES
    rows = slots // STAGES
    n_t = chips * CORES
    sent = len(cuts(feats))
    bf16, f32 = jnp.bfloat16, jnp.float32
    late = chips // 2 * (STAGES - EARLY) * CORES * rows
    wide = 512

    def cut(array):
        return array.reshape(STAGES, rows, array.shape[1])

    hbm = pl.BlockSpec(memory_space=pl.ANY)
    vmem = pl.BlockSpec(memory_space=pltpu.VMEM)
    dma = pltpu.SemaphoreType.DMA
    summed, dg, du, pg, pu, xt, kg, ku = pl.pallas_call(
        gather_kernel,
        out_shape=(
            jax.ShapeDtypeStruct((STAGES, rows, feats), bf16),
            jax.ShapeDtypeStruct((STAGES - EARLY, CORES, rows, ff), bf16),
            jax.ShapeDtypeStruct((STAGES - EARLY, CORES, rows, ff), bf16),
            jax.ShapeDtypeStruct((feats, ff), bf16),
            jax.ShapeDtypeStruct((feats, ff), bf16),
            jax.ShapeDtypeStruct((feats, late), bf16),
            jax.ShapeDtypeStruct((feats // BLK, ff), f32),
            jax.ShapeDtypeStruct((feats // BLK, ff), f32),
        ),
        in_specs=[hbm] * 6 + [vmem] * 2 + [pl.BlockSpec(memory_space=pltpu.SMEM)],
        out_specs=(vmem, hbm, hbm, hbm, hbm, vmem, vmem, vmem),
        scratch_shapes=[
            pltpu.VMEM((chips, STAGES, CORES, rows, ff), bf16),
            pltpu.VMEM((chips, STAGES, CORES, rows, ff), bf16),
            pltpu.VMEM((feats, ff), bf16),
            pltpu.VMEM((feats, ff), bf16),
            pltpu.VMEM((STAGES, rows, ff), bf16),
            pltpu.VMEM((STAGES, rows, ff), bf16),
            pltpu.VMEM((STAGES, rows, ff), bf16),
            pltpu.VMEM((chips, STAGES, CORES, rows, feats), bf16),
            pltpu.VMEM((feats, n_t * slots - late), bf16),
            pltpu.VMEM((2, feats, wide), bf16),
            pltpu.VMEM((chips, STAGES, CORES, rows, feats), bf16),
            pltpu.VMEM((n_t, STAGES, rows, feats), bf16),
            dma((STAGES, 3)), dma((2,)), dma, dma((n_t - 1,)), dma((n_t - 1,)),
            dma((STAGES, 2)), dma((STAGES, 2)), dma((STAGES, 2)), dma((STAGES, 2)),
            dma((STAGES, 2)), dma((STAGES, 2)), dma((STAGES - EARLY, 2)), dma((2, 2)),
            dma((n_t, sent)), dma((n_t, sent)),
        ],
        compiler_params=pltpu.CompilerParams(
            collective_id=0, has_side_effects=True, vmem_limit_bytes=VMEM_LIMIT
        ),
        name="gather_and_input_grad",
    )(
        cut(layer_input), cut(gate_pre), cut(up_pre), cut(d_hidden),
        w_gate, w_up, mask_gate, mask_up, lengths,
    )
    wide = 1024
    grad_w_gate, grad_w_up = pl.pallas_call(
        weight_kernel,
        grid=(ff // wide,),
        out_shape=(jax.ShapeDtypeStruct((feats, ff), bf16),) * 2,
        in_specs=[
            pl.BlockSpec((feats, late), lambda j: (0, 0)),
            pl.BlockSpec((late, wide), lambda j: (0, j)),
            pl.BlockSpec((late, wide), lambda j: (0, j)),
            pl.BlockSpec((feats, wide), lambda j: (0, j)),
            pl.BlockSpec((feats, wide), lambda j: (0, j)),
            pl.BlockSpec((feats // BLK, wide), lambda j: (0, j)),
            pl.BlockSpec((feats // BLK, wide), lambda j: (0, j)),
        ],
        out_specs=(pl.BlockSpec((feats, wide), lambda j: (0, j)),) * 2,
        compiler_params=pltpu.CompilerParams(vmem_limit_bytes=VMEM_LIMIT),
        name="weight_grads",
    )(xt, dg.reshape(late, ff), du.reshape(late, ff), pg, pu, kg, ku)
    return summed.reshape(slots, feats), grad_w_gate, grad_w_up


def expand(mask):
    return jnp.repeat(jnp.repeat(mask, BLK, axis=0), BLK, axis=1)


def swiglu_back(gate, upper, grad, keep):
    g = gate.astype(jnp.float32)
    sig = jax.nn.sigmoid(g)
    err = jnp.where(keep[:, None], grad.astype(jnp.float32), jnp.float32(0.0))
    d_up = err * g * sig
    d_gate = err * upper.astype(jnp.float32) * sig * (1.0 + g * (1.0 - sig))
    return (d_gate.astype(jnp.bfloat16), d_up.astype(jnp.bfloat16))


def local(layer_input, gate_pre, up_pre, d_hidden, w_gate, w_up, mask_gate, mask_up, lengths):
    group = lax.axis_index("dp")
    slots_dev = gate_pre.shape[0]
    keep_gate = expand(mask_gate).astype(jnp.bfloat16)
    keep_up = expand(mask_up).astype(jnp.bfloat16)
    gate_eff = w_gate * keep_gate
    up_eff = w_up * keep_up
    inner = (((1,), (1,)), ((), ()))
    input_all = lax.all_gather(layer_input, "tensor", axis=0, tiled=True)
    keep = jnp.arange(slots_dev) < lengths[group]
    d_gate, d_up = swiglu_back(gate_pre, up_pre, d_hidden, keep)
    gate_all, up_all = (
        lax.all_gather(d_gate, "dp", axis=0, tiled=True),
        lax.all_gather(d_up, "dp", axis=0, tiled=True),
    )
    term = lax.dot_general(gate_all, gate_eff, inner, preferred_element_type=jnp.float32)
    summed = lax.psum_scatter(
        (term + lax.dot_general(up_all, up_eff, inner, preferred_element_type=jnp.float32)).astype(
            jnp.bfloat16
        ),
        "tensor",
        scatter_dimension=0,
        tiled=True,
    )
    contract = (((0,), (0,)), ((), ()))
    grad_w_gate = lax.dot_general(input_all, gate_all, contract, preferred_element_type=jnp.float32)
    grad_w_gate = (grad_w_gate * keep_gate.astype(jnp.float32)).astype(jnp.bfloat16)
    grad_w_up = lax.dot_general(input_all, up_all, contract, preferred_element_type=jnp.float32)
    grad_w_up = (grad_w_up * keep_up.astype(jnp.float32)).astype(jnp.bfloat16)
    return (summed, grad_w_gate, grad_w_up)


def solution(mesh):
    placed = (
        P(("parts", "tensor"), "dp"),
        P(("parts", "dp"), "tensor"),
        P(("parts", "dp"), "tensor"),
        P(("parts", "dp"), "tensor"),
        P("dp", "tensor"),
        P("dp", "tensor"),
        P("dp", "tensor"),
        P("dp", "tensor"),
        P("parts"),
    )
    paired = mesh.shape["dp"] == 2 * CORES and mesh.shape["tensor"] == mesh.shape["dp"]
    return jax.shard_map(
        staged if paired else local,
        mesh=mesh,
        in_specs=placed,
        out_specs=(
            P(("parts", "tensor"), "dp"),
            P(("parts", "dp"), "tensor"),
            P(("parts", "dp"), "tensor"),
        ),
        check_vma=False,
    )
```
